32 devices in a mesh: groups: 4 (over y, x), shard: 8 (over z, core).
Axes of the slice: x: 2, y: 2, z: 4, core: 2. Of those that a mesh axis runs over, the one named last changes fastest.
Arguments:
- gradients: bfloat16 [4, 96, 1024, 1024], P('groups', None, 'shard'), may hold values from -200 to 200
- second_moment: bfloat16 [96, 1024, 1024], P('groups', 'shard'), may hold values from 0.25 to 4
- inverse_roots: bfloat16 [4, 8, 6, 2, 1024, 1024], P('groups', 'shard'), may hold values from -2 to 2
- owners: int32 [96], replicated, may hold values from 0 to 7, as said below
- weights: bfloat16 [96, 1024, 1024], P('groups', 'shard'), may hold values from -4 to 4
Outputs:
- new_weights: bfloat16 [96, 1024, 1024], P(None, 'shard')
The draws below stay inside these ranges and needn't reach their ends.
Inputs may be any that keep to these rules, and one draw needn't show every extreme that they name: `owners`: blocks 24 * g to 24 * (g + 1) - 1 form group g. Within a group no owner is named by more than 6 blocks, and some owner is named by exactly 6.
All inputs are finite; a program needn't handle non-finite values.
Results may differ from the reference program's by a relative error of at most 0.0004.
The reference program's roundings to bfloat16 on the way (of `update`) count: a program that leaves them out, or rounds other values in their place, can miss the bound.
Values may be sent and summed in bfloat16 or wider, within the bound.
A program may use at most 256 MiB of HBM per device.

```python
import math
import jax
import jax.numpy as jnp
from jax import lax

BLOCK = 1024
NB = 96
NBG = 24
MOST = 6
N_GROUPS = 4
N_SHARD = 8


def draw_gradients(key, part):
    k_entries, k_row, k_col = jax.random.split(key, 3)
    row_scale = jnp.exp(jax.random.uniform(k_row, (NB, BLOCK, 1), jnp.float32, 0.0, math.log(10.0)))
    col_scale = jnp.exp(jax.random.uniform(k_col, (NB, 1, BLOCK), jnp.float32, 0.0, math.log(10.0)))
    position = jnp.arange(BLOCK, dtype=jnp.float32).reshape(1, BLOCK, 1) / BLOCK
    entries = jnp.clip(jax.random.normal(k_entries, (N_GROUPS, NB, BLOCK, BLOCK), jnp.float32), -4.0, 4.0)
    rising = jnp.exp(position * math.log(3.0))
    return (0.03 * entries * (row_scale * rising * col_scale)[None]).astype(jnp.bfloat16)


def draw_inverse_roots(key, part):
    k_diag, k_spread = jax.random.split(jax.random.fold_in(key, 11), 2)
    shape_all = (N_GROUPS, N_SHARD, MOST, 2, BLOCK, BLOCK)
    diagonal = jnp.exp(jax.random.uniform(k_diag, (N_GROUPS, N_SHARD, MOST, 2, BLOCK, 1), jnp.float32, math.log(0.5), math.log(2.0)))
    sigma = 0.5 / math.sqrt(BLOCK)
    spread_part = jnp.clip(jax.random.normal(k_spread, shape_all, jnp.float32), -4.0, 4.0) * sigma
    on_diagonal = jnp.arange(BLOCK)[:, None] == jnp.arange(BLOCK)[None, :]
    return jnp.where(on_diagonal, diagonal, spread_part).astype(jnp.bfloat16)


def draw_owners(key, part):

    def one_group(group_key):
        k_first, k_order, k_place = jax.random.split(group_key, 3)
        first_owner = jax.random.randint(k_first, (), 0, N_SHARD)
        slot_ids = jnp.arange(N_SHARD * MOST, dtype=jnp.int32)
        owner_of = slot_ids // MOST
        order_score = jax.random.permutation(k_order, N_SHARD * MOST).astype(jnp.int32)
        order_score = jnp.where(owner_of == first_owner, -1 - slot_ids % MOST, order_score)
        ranking = jnp.argsort(order_score, stable=True)
        chosen = owner_of[ranking[:NBG]]
        return chosen[jax.random.permutation(k_place, NBG)]
    group_keys = jax.random.split(jax.random.fold_in(key, 7), N_GROUPS)
    return jax.vmap(one_group)(group_keys).reshape(NB).astype(jnp.int32)


def shard_levels(own_key, dims, cuts, smallest, high):
    gain, own = 1.0, jax.random.fold_in(own_key, 6)
    for dim, parts in cuts:
        steps = jnp.exp(jax.random.uniform(jax.random.fold_in(own, dim), (parts,), jnp.float32, smallest / len(cuts), high / len(cuts)))
        gain = gain * jnp.repeat(steps, dims[dim] // parts).reshape([-1 if axis == dim else 1 for axis in range(len(dims))])
    return gain


def centred(rng, dims, width, bound, pieces=(), held_as=jnp.bfloat16):
    array = width * jax.random.normal(rng, dims, jnp.float32)
    if pieces:
        array = array * shard_levels(rng, dims, pieces, -0.22, 0.18)
    return jnp.clip(array, -bound, bound).astype(held_as)


def setup_inputs(seed: int = 0) -> dict:
    seeds = jax.random.split(jax.random.key(seed), 6)
    gradients = draw_gradients(jax.random.fold_in(seeds[5], 71), 0)
    second_moment = jnp.clip(jnp.exp(math.log(4.0) - 2.7725887 * jax.random.uniform(seeds[1], (NB, BLOCK, BLOCK), jnp.float32) ** shard_levels(seeds[1], (NB, BLOCK, BLOCK), ((0, 4), (1, 8)), -0.2, 0.2)), 0.25, 4.0).astype(jnp.bfloat16)
    inverse_roots = draw_inverse_roots(jax.random.fold_in(seeds[5], 71), 0)
    owners = draw_owners(jax.random.fold_in(seeds[5], 71), 0)
    weights = centred(seeds[4], (NB, BLOCK, BLOCK), 1.0, 4.0, ((0, 4), (1, 8)))
    return {"gradients": gradients, "second_moment": second_moment, "inverse_roots": inverse_roots, "owners": owners, "weights": weights}


def reference(gradients, second_moment, inverse_roots, owners, weights):
    total = lax.optimization_barrier(jnp.sum(gradients.astype(jnp.float32), axis=0))
    grouped = owners.reshape(N_GROUPS, NBG)
    same_owner = grouped[:, :, None] == grouped[:, None, :]
    earlier = jnp.arange(NBG)[None, :] < jnp.arange(NBG)[:, None]
    rank = lax.optimization_barrier(jnp.sum(same_owner & earlier[None], axis=2)).reshape(NB).astype(jnp.int32)
    group_ids = (jnp.arange(NB) // NBG).astype(jnp.int32)

    def update_block(items):
        block_grad, moment_old, block_weights, owner, slot, group = items
        moment = 0.95 * moment_old.astype(jnp.float32) + 0.05 * block_grad * block_grad
        adam_step = block_grad / (jnp.sqrt(moment) + 1e-08)
        graft_sq = jnp.sum(adam_step * adam_step)
        left_root = inverse_roots[group, owner, slot, 0].astype(jnp.float32)
        right_root = inverse_roots[group, owner, slot, 1].astype(jnp.float32)
        right_product = jnp.dot(block_grad, right_root, precision=lax.Precision.HIGHEST, preferred_element_type=jnp.float32)
        preconditioned = jnp.dot(left_root, right_product, precision=lax.Precision.HIGHEST, preferred_element_type=jnp.float32)
        graft_scale = jnp.sqrt(graft_sq) / jnp.sqrt(jnp.sum(preconditioned * preconditioned) + 1e-06)
        update = lax.optimization_barrier((graft_scale * preconditioned).astype(jnp.bfloat16))
        stepped = block_weights.astype(jnp.float32) - 0.5 * update.astype(jnp.float32)
        renormed = stepped * lax.rsqrt(lax.optimization_barrier(jnp.mean(stepped * stepped, axis=1, keepdims=True)) + 1e-06)
        return renormed.astype(jnp.bfloat16)
    return lax.map(update_block, (total, second_moment, weights, owners, rank, group_ids))
```

```python
import jax
import jax.numpy as jnp
from jax import lax
from jax.experimental import pallas as pl
from jax.experimental.pallas import tpu as pltpu
from jax.sharding import PartitionSpec as P


def split(value):
    high = lax.reduce_precision(value, 8, 7)
    low = value - high
    return high.astype(jnp.bfloat16), low.astype(jnp.bfloat16)


def product(left, right):
    return jnp.einsum(
        "mij,mjk->mik", left, right, preferred_element_type=jnp.float32
    )


def pack_kernel(order, present, replicas, moments, packed, squares):
    slot = pl.program_id(0)
    total = replicas[0, 0].astype(jnp.float32)
    for replica in range(1, replicas.shape[0]):
        total = total + replicas[replica, 0].astype(jnp.float32)
    total = jnp.where(present[slot] > 0, total, 0.0)
    high = total.astype(jnp.bfloat16)
    packed[0, 0] = high
    packed[1, 0] = (total - high.astype(jnp.float32)).astype(jnp.bfloat16)
    moment = 0.95 * moments[0].astype(jnp.float32) + 0.05 * total * total
    adam_step = total / (jnp.sqrt(moment) + 1e-08)
    square = adam_step * adam_step
    rows, width = square.shape
    squares[0] = jnp.sum(square.reshape(rows // 8, 8, width), axis=0)


def pack(order, present, replicas, moments):
    groups, _, rows, width = replicas.shape
    slots = order.shape[0]
    return pl.pallas_call(
        pack_kernel,
        grid_spec=pltpu.PrefetchScalarGridSpec(
            num_scalar_prefetch=2,
            grid=(slots,),
            in_specs=[
                pl.BlockSpec((groups, 1, rows, width), lambda s, o, p: (0, o[s], 0, 0)),
                pl.BlockSpec((1, rows, width), lambda s, o, p: (o[s], 0, 0)),
            ],
            out_specs=[
                pl.BlockSpec((2, 1, rows, width), lambda s, o, p: (0, s, 0, 0)),
                pl.BlockSpec((1, 8, width), lambda s, o, p: (s, 0, 0)),
            ],
        ),
        out_shape=[
            jax.ShapeDtypeStruct((2, slots, rows, width), jnp.bfloat16),
            jax.ShapeDtypeStruct((slots, 8, width), jnp.float32),
        ],
        compiler_params=pltpu.CompilerParams(vmem_limit_bytes=24 * 1024 * 1024),
    )(order, present, replicas, moments)


def step_kernel(place, returned, weights, renormed):
    stepped = weights[0].astype(jnp.float32) - 0.5 * returned[0].astype(jnp.float32)
    mean = jnp.mean(stepped * stepped, axis=1, keepdims=True)
    renormed[0] = (stepped * lax.rsqrt(mean + 1e-06)).astype(jnp.bfloat16)


def step(place, returned, weights):
    blocks, rows, width = weights.shape
    return pl.pallas_call(
        step_kernel,
        grid_spec=pltpu.PrefetchScalarGridSpec(
            num_scalar_prefetch=1,
            grid=(blocks,),
            in_specs=[
                pl.BlockSpec((1, rows, width), lambda b, p: (p[b], 0, 0)),
                pl.BlockSpec((1, rows, width), lambda b, p: (b, 0, 0)),
            ],
            out_specs=pl.BlockSpec((1, rows, width), lambda b, p: (b, 0, 0)),
        ),
        out_shape=jax.ShapeDtypeStruct(weights.shape, jnp.bfloat16),
        compiler_params=pltpu.CompilerParams(vmem_limit_bytes=24 * 1024 * 1024),
    )(place, returned, weights)


def body(gradients, second_moment, inverse_roots, owners, weights):
    groups_count = lax.axis_size("groups")
    shard_count = lax.axis_size("shard")
    group_index = lax.axis_index("groups")
    shard_index = lax.axis_index("shard")
    total_blocks = owners.shape[0]
    per_group = total_blocks // groups_count
    slot_count = inverse_roots.shape[2]
    row_count = gradients.shape[2]
    block_width = gradients.shape[3]
    group_start = group_index * per_group

    local_owner = lax.dynamic_slice_in_dim(owners, group_start, per_group, 0)
    same_owner = local_owner[:, None] == local_owner[None, :]
    block_ids = jnp.arange(per_group, dtype=jnp.int32)
    earlier = block_ids[None, :] < block_ids[:, None]
    position = jnp.sum(same_owner & earlier, axis=1).astype(jnp.int32)
    slot_ids = jnp.arange(slot_count, dtype=jnp.int32)
    dest_ids = jnp.arange(shard_count, dtype=jnp.int32)
    slot_match = (local_owner[None, None, :] == dest_ids[None, :, None]) & (
        position[None, None, :] == slot_ids[:, None, None]
    )
    present = jnp.any(slot_match, axis=2).astype(jnp.int32).reshape(-1)
    order = jnp.sum(jnp.where(slot_match, block_ids[None, None, :], 0), axis=2)
    order = order.astype(jnp.int32).reshape(-1)

    replicas = lax.all_to_all(
        gradients.reshape(groups_count, per_group, row_count, block_width),
        "groups",
        split_axis=0,
        concat_axis=0,
        tiled=True,
    )
    packed, squares = pack(order, present, replicas, second_moment)
    graft_all = lax.psum(jnp.sum(squares, axis=(1, 2)), "shard")
    graft_sq = lax.dynamic_index_in_dim(
        graft_all.reshape(slot_count, shard_count), shard_index, 1, keepdims=False
    )
    outgoing = packed.reshape(2, slot_count, shard_count, row_count, block_width)
    arrived = lax.all_to_all(outgoing, "shard", split_axis=2, concat_axis=2, tiled=True)
    arrived = arrived.reshape(2, slot_count, block_width, block_width)
    roots_mine = inverse_roots[0, 0]
    left, right = roots_mine[:, 0], roots_mine[:, 1]
    right_product = product(arrived[0], right) + product(arrived[1], right)
    high, low = split(right_product)
    preconditioned = product(left, high) + product(left, low)
    graft_scale = jnp.sqrt(graft_sq) / jnp.sqrt(
        jnp.sum(preconditioned * preconditioned, axis=(1, 2)) + 1e-06
    )
    update = (graft_scale[:, None, None] * preconditioned).astype(jnp.bfloat16)
    update = update.reshape(slot_count, shard_count, row_count, block_width)
    returned = lax.all_to_all(update, "shard", split_axis=1, concat_axis=1, tiled=True)
    returned = returned.reshape(slot_count * shard_count, row_count, block_width)
    renormed = step(position * shard_count + local_owner, returned, weights)
    return lax.all_gather(renormed, "groups", axis=0, tiled=True)


def solution(mesh):
    return jax.shard_map(
        body,
        mesh=mesh,
        in_specs=(
            P("groups", None, "shard", None),
            P("groups", "shard", None),
            P("groups", "shard", None, None, None, None),
            P(),
            P("groups", "shard", None),
        ),
        out_specs=P(None, "shard", None),
        check_vma=False,
    )
```

```python
import jax
import jax.numpy as jnp
from jax import lax
from jax.experimental import pallas as pl
from jax.experimental.pallas import tpu as pltpu
from jax.sharding import PartitionSpec as P


def split(value):
    high = lax.reduce_precision(value, 8, 7)
    low = value - high
    return high.astype(jnp.bfloat16), low.astype(jnp.bfloat16)


def product(left, right):
    return jnp.dot(left, right, preferred_element_type=jnp.float32)


def call(kernel, table, steps, ins, outs):
    return pl.pallas_call(
        kernel,
        grid_spec=pltpu.PrefetchScalarGridSpec(
            num_scalar_prefetch=1,
            grid=(steps,),
            in_specs=[pl.BlockSpec(shape, index) for _, shape, index in ins],
            out_specs=[pl.BlockSpec((1,) + o.shape[1:], lambda s, t: (s, 0, 0)) for o in outs],
        ),
        out_shape=outs,
        compiler_params=pltpu.CompilerParams(vmem_limit_bytes=32 * 1024 * 1024),
    )(table, *[array for array, _, _ in ins])


def choose(table, stride, sources):
    tile = (1,) + sources[0].shape[-2:]

    def index_of(column):
        def index(s, t):
            return (jnp.where(t[stride * s] == column, t[stride * s + 1], 0), 0, 0)
        return index

    return [(source, tile, index_of(column)) for column, source in enumerate(sources)]


def reorder(table, array):
    tile = (1,) + array.shape[1:]

    def kernel(t, source, out):
        out[...] = source[...]

    out = jax.ShapeDtypeStruct(table.shape + array.shape[1:], array.dtype)
    return call(
        kernel, table, table.shape[0], [(array, tile, lambda s, t: (t[s], 0, 0))], [out]
    )[0]


def pack(table, steps, chunks, moments):
    groups = len(chunks[0])
    _, rows, width = chunks[0][0].shape

    def kernel(t, *refs):
        sources, moment_ref, packed, squares = refs[:-3], refs[-3], refs[-2], refs[-1]
        part = t[3 * pl.program_id(0)]

        @pl.when(part < 0)
        def _():
            packed[...] = jnp.zeros_like(packed)

        for column in range(len(chunks)):

            @pl.when(part == column)
            def _(column=column):
                total = sources[column * groups][0].astype(jnp.float32)
                for replica in range(1, groups):
                    total = total + sources[column * groups + replica][0].astype(jnp.float32)
                packed[0] = total

        total = packed[0]
        moment = 0.95 * moment_ref[0].astype(jnp.float32) + 0.05 * total * total
        adam_step = total / (jnp.sqrt(moment) + 1e-08)
        square = adam_step * adam_step
        squares[0] = jnp.sum(square.reshape(rows // 8, 8, width), axis=0)

    def index_of(column):
        def index(s, t):
            return (jnp.where(t[3 * s] == column, t[3 * s + 1], 0), 0, 0)
        return index

    ins = [(a, (1, rows, width), index_of(i)) for i, c in enumerate(chunks) for a in c]
    ins.append((moments, (1, rows, width), lambda s, t: (t[3 * s + 2], 0, 0)))
    outs = [
        jax.ShapeDtypeStruct((steps, rows, width), jnp.float32),
        jax.ShapeDtypeStruct((steps, 8, width), jnp.float32),
    ]
    return call(kernel, table, steps, ins, outs)


def step(table, steps, returned, weights):
    tile = (1,) + weights.shape[1:]

    def kernel(t, *refs):
        sources, weight, out = refs[:-2], refs[-2], refs[-1]
        part = t[3 * pl.program_id(0)]
        for column, source in enumerate(sources):

            @pl.when(part == column)
            def _(source=source):
                stepped = weight[0].astype(jnp.float32) - 0.5 * source[0].astype(jnp.float32)
                mean = jnp.mean(stepped * stepped, axis=1, keepdims=True)
                out[0] = (stepped * lax.rsqrt(mean + 1e-06)).astype(jnp.bfloat16)

    ins = choose(table, 3, returned)
    ins.append((weights, tile, lambda s, t: (t[3 * s + 2], 0, 0)))
    return call(kernel, table, steps, ins, [jax.ShapeDtypeStruct((steps,) + tile[1:], jnp.bfloat16)])[0]


def collect(table, steps, gathered):
    def kernel(t, *refs):
        sources, out = refs[:-1], refs[-1]
        part = t[2 * pl.program_id(0)]
        for column, source in enumerate(sources):

            @pl.when(part == column)
            def _(source=source):
                out[...] = source[...]

    out = jax.ShapeDtypeStruct((steps,) + gathered[0].shape[1:], gathered[0].dtype)
    return call(kernel, table, steps, choose(table, 2, gathered), [out])[0]


def body(gradients, second_moment, inverse_roots, owners, weights):
    groups = lax.axis_size("groups")
    shards = lax.axis_size("shard")
    group = lax.axis_index("groups")
    blocks = owners.shape[0] // groups
    slots = inverse_roots.shape[2]
    rows, width = gradients.shape[2:]

    grouped = owners.reshape(groups, blocks)
    ids = jnp.arange(blocks, dtype=jnp.int32)
    same = grouped[:, :, None] == grouped[:, None, :]
    rank = jnp.sum(same & (ids[None, :] < ids[:, None])[None], axis=2).astype(jnp.int32)
    key = rank * shards + grouped
    place = jnp.sum(key[:, None, :] < key[:, :, None], axis=2).astype(jnp.int32)
    taken = place[:, None, :] == ids[None, :, None]
    block_at = jnp.sum(jnp.where(taken, ids, 0), axis=2).astype(jnp.int32)

    def mine(array):
        return lax.dynamic_index_in_dim(array, group, 0, keepdims=False)

    my_key, my_place, my_block = mine(key), mine(place), mine(block_at)
    key_at = jnp.sum(jnp.where(mine(taken), my_key, 0), axis=1).astype(jnp.int32)

    chunk_in = min(blocks, shards)
    cuts = [(a, min(a + chunk_in, blocks)) for a in range(0, blocks, chunk_in)]
    first = jnp.arange(groups, dtype=jnp.int32)[:, None] * blocks
    chunks = []
    for low, high in cuts:
        ordered = reorder((first + block_at[:, low:high]).reshape(-1), gradients[0])
        ordered = ordered.reshape(groups, high - low, rows, width)
        received = [lax.dynamic_index_in_dim(ordered, group, 0, keepdims=False)]
        for shift in range(1, groups):
            sent = lax.dynamic_index_in_dim(
                ordered, lax.rem(group + shift, groups), 0, keepdims=False
            )
            pairs = [(g, (g + shift) % groups) for g in range(groups)]
            received.append(lax.ppermute(sent, "groups", pairs))
        chunks.append(received)

    parts = 3 if slots % 3 == 0 and blocks % 3 == 0 else 1
    chunk_out = blocks // parts
    returned, gathered, renormed = [], [], []

    def exchange(array):
        return lax.all_to_all(array, "shard", split_axis=0, concat_axis=0, tiled=True)

    def send(slot, after):
        wanted = my_key[None, :] == (slot * shards + jnp.arange(shards, dtype=jnp.int32))[:, None]
        present = jnp.any(wanted, axis=1)
        at = jnp.sum(jnp.where(wanted, my_place, 0), axis=1).astype(jnp.int32)
        source = jnp.sum(jnp.where(wanted, ids, 0), axis=1).astype(jnp.int32)
        table = jnp.stack(
            [jnp.where(present, at // chunk_in, -1), at % chunk_in, source], axis=1
        ).reshape(-1)
        packed, squares = pack(table, shards, chunks[: slot + 1], second_moment)
        squares = jnp.sum(squares, axis=1, keepdims=True)
        packed, squares, _ = lax.optimization_barrier((packed, squares, after))
        return exchange(packed), exchange(squares)

    def compute(slot, arrived, squares):
        high, low = split(arrived.reshape(shards * rows, width))
        left, right = inverse_roots[0, 0, slot, 0], inverse_roots[0, 0, slot, 1]
        right_product = product(high, right) + product(low, right)
        high, low = split(right_product)
        preconditioned = product(left, high) + product(left, low)
        scale = jnp.sqrt(jnp.sum(squares)) / jnp.sqrt(
            jnp.sum(preconditioned * preconditioned) + 1e-06
        )
        return (scale * preconditioned).astype(jnp.bfloat16).reshape(shards, rows, width)

    arrived, squares = send(0, ())
    for slot in range(slots):
        if slot + 1 < slots:
            after = (arrived, returned[-1:], renormed[-1:])
            following = send(slot + 1, after)
            update = compute(slot, arrived, squares)
            update, arrived = lax.optimization_barrier((update, following[0]))
            squares = following[1]
        else:
            update = compute(slot, arrived, squares)
        returned.append(exchange(update))
        if (slot + 1) * parts % slots == 0:
            start = len(gathered) * chunk_out
            keys = key_at[start : start + chunk_out]
            table = jnp.stack(
                [keys // shards, keys % shards, my_block[start : start + chunk_out]], axis=1
            ).reshape(-1)
            renormed.append(step(table, chunk_out, returned, weights))
            gathered.append(lax.all_gather(renormed[-1], "groups", axis=0, tiled=True))

    inner = jnp.arange(groups, dtype=jnp.int32)[:, None] * chunk_out + place % chunk_out
    table = jnp.stack([place // chunk_out, inner], axis=2).reshape(-1)
    return collect(table, groups * blocks, gathered)


def solution(mesh):
    return jax.shard_map(
        body,
        mesh=mesh,
        in_specs=(
            P("groups", None, "shard", None),
            P("groups", "shard", None),
            P("groups", "shard", None, None, None, None),
            P(),
            P("groups", "shard", None),
        ),
        out_specs=P(None, "shard", None),
        check_vma=False,
    )
```
